32 devices in a mesh: row: 4 (over y, x), col: 8 (over z, core).
Axes of the slice: x: 2, y: 2, z: 4, core: 2. Of those that a mesh axis runs over, the one named last changes fastest.
Arguments:
- multiplier: float32 [512, 20480], P(('row', 'col')), may hold values from -6 to 6
- cycle_tiles: float32 [20480, 512], P('row', 'col'), may hold values from -0.0625 to 0.0625
Outputs:
- symmetric: float32 [512, 512], P(('row', 'col'))
The draws below stay inside these ranges and needn't reach their ends.
All inputs are finite; a program needn't handle non-finite values.
Results may differ from the reference program's by a relative error of at most 0.00007.
Values sent between devices are 32-bit elements; how exact they have to be, the bound alone decides.
A program may use at most 64 MiB of HBM per device.

```python
import jax
import jax.numpy as jnp
from jax import lax

O = 40
V = 512
OW = 1
ROWS = 512
JW = 512
K = 20480
N_ROW = 4
N_COL = 8


def with_spikes(drawn, rng, source, target, shards_of, factor):
    owner, partner = [(jnp.arange(drawn.shape[dim]) // (drawn.shape[dim] // shards_of)).reshape([-1 if axis == dim else 1 for axis in range(drawn.ndim)]) for dim in (source, target)]
    chosen = jax.random.permutation(rng, shards_of)[partner]
    strong = (owner == chosen) | (owner == (partner + shards_of // 2) % shards_of)
    return jnp.where(strong, factor * drawn, drawn)


def block_levels(rng, dims, shards, least, largest):
    loudness = 1.0
    for position, parts in shards:
        draws = jax.random.uniform(jax.random.fold_in(jax.random.fold_in(rng, 6), position), (parts,), jnp.float32, least / len(shards), largest / len(shards))
        loudness = loudness * jnp.repeat(jnp.exp(draws), dims[position] // parts).reshape((-1,) + (1,) * (len(dims) - 1 - position))
    return loudness


def noise(key, extent, scale, reach, cuts=(), dtype=jnp.bfloat16):
    entries = jax.random.normal(key, extent, jnp.float32) * scale
    if len(cuts) > 0:
        entries = block_levels(key, extent, cuts, -0.22, 0.18) * entries
    return jnp.clip(entries, min=-reach, max=reach).astype(dtype)


def heavy_noise(own_key, extent, width, reach, pieces, heavy, held_as=jnp.bfloat16):
    result = width * jax.random.normal(own_key, extent, jnp.float32)
    if pieces:
        result = result * block_levels(own_key, extent, pieces, -0.22, 0.18)
    return jnp.clip(with_spikes(result, jax.random.fold_in(own_key, 3), *heavy), -reach, reach).astype(held_as)


def setup_inputs(seed: int = 0) -> dict:
    seeds = jax.random.split(jax.random.key(seed), 3)
    multiplier = noise(seeds[0], (ROWS, K), 1.0, 6.0, ((0, 32),), jnp.float32)
    cycle_tiles = heavy_noise(seeds[1], (K, JW), K ** -0.5, 0.0625, ((0, 4), (1, 8)), (0, 1, 8, 2.0), jnp.float32)
    return dict(multiplier=multiplier, cycle_tiles=cycle_tiles)


def reference(multiplier, cycle_tiles):
    block_width = JW // (N_ROW * N_COL)
    cycle_full = jnp.transpose(cycle_tiles.reshape(K, N_COL, N_ROW, block_width), (0, 2, 1, 3)).reshape(K, JW)
    swapped = jnp.transpose(multiplier.reshape(V, OW, V, O), (2, 1, 0, 3)).reshape(ROWS, K)
    combined = 2.0 * multiplier - swapped
    cycle_term = jnp.dot(combined, cycle_full, precision=lax.Precision.HIGHEST, preferred_element_type=jnp.float32)
    mirror = jnp.transpose(cycle_term.reshape(V, OW, V, OW), (2, 1, 0, 3)).reshape(ROWS, JW)
    return cycle_term + mirror
```

```python
import jax
import jax.numpy as jnp
from jax import lax
from jax.sharding import PartitionSpec as P

O = 40
V = 512
OW = 1


def on_device(multiplier, cycle_tiles):
    rows_loc, full_width = multiplier.shape
    row_count = lax.axis_size("row")
    col_count = lax.axis_size("col")
    devices = row_count * col_count
    block_width = full_width // devices
    out_block = cycle_tiles.shape[1] // row_count
    virt_dev = rows_loc // OW
    all_rows = rows_loc * devices
    pieces = multiplier.reshape(1, rows_loc, devices, block_width)
    moved = lax.all_to_all(pieces, ("row", "col"), split_axis=2, concat_axis=0, tiled=True)
    direct = moved.reshape(all_rows, block_width)
    cycle_rows = lax.all_to_all(cycle_tiles.T, "col", split_axis=1, concat_axis=0, tiled=True)
    swapped = jnp.transpose(multiplier.reshape(virt_dev, OW, V, O), (2, 1, 0, 3)).reshape(
        all_rows, block_width
    )
    combined = 2.0 * direct - swapped
    partial_value = lax.dot_general(
        cycle_rows,
        combined,
        (((1,), (1,)), ((), ())),
        precision=lax.Precision.HIGHEST,
        preferred_element_type=jnp.float32,
    )
    partial_value = partial_value.reshape(col_count, row_count, out_block, all_rows)
    over_row = lax.psum_scatter(partial_value, "row", scatter_dimension=1, tiled=True)
    own_cols = lax.psum_scatter(over_row, "col", scatter_dimension=0, tiled=True)
    own_cols = own_cols.reshape(out_block, all_rows)
    outgoing = own_cols.reshape(1, out_block, devices, rows_loc)
    arrived = lax.all_to_all(outgoing, ("row", "col"), split_axis=2, concat_axis=0, tiled=True)
    own_rows = arrived.reshape(devices * out_block, rows_loc).T
    return own_rows + own_cols


def solution(mesh):
    placed = (P(("row", "col"), None), P("row", "col"))
    return jax.shard_map(
        on_device, mesh=mesh, in_specs=placed, out_specs=P(("row", "col"), None), check_vma=False
    )
```

```python
import functools

import jax
import jax.numpy as jnp
from jax import lax
from jax.experimental import pallas as pl
from jax.experimental.pallas import tpu as pltpu
from jax.sharding import PartitionSpec as P

O = 40
V = 512
OW = 1
MESH = pl.DeviceIdType.MESH


def flip(x, y, size):
    total, bit = 0, 1
    while bit < size:
        total = total + bit * ((x // bit + y // bit) % 2)
        bit *= 2
    return total


def halves(x):
    high = x.astype(jnp.bfloat16)
    return high, (x - high.astype(jnp.float32)).astype(jnp.bfloat16)


def dot_nt(x, y):
    return lax.dot_general(
        x, y, (((1,), (1,)), ((), ())), preferred_element_type=jnp.float32
    )


def cycle_kernel(
    rows, cols, t_ref, w_ref, out_ref,
    wt, tdir, u, sw, dh, dl, wr, pbuf, rbuf, qbuf, cbuf, qt, mbuf,
    t_send, t_recv, w_send, w_recv, r_send, r_recv, c_send, c_recv, m_send, m_recv,
):
    n = rows * cols
    own, width = t_ref.shape
    block = width // n
    chunk = w_ref.shape[1]
    count = own * n
    r = lax.axis_index("row")
    c = lax.axis_index("col")
    me = r * cols + c

    def partner(step):
        s, q = step % cols, step // cols
        pr = flip(r, (q + s) % rows, rows)
        pc = flip(c, (s % 2) * (cols // 2) + s // 2, cols)
        return pr, pc, pr * cols + pc

    barrier = pltpu.get_barrier_semaphore()

    @pl.loop(1, n)
    def _(step):
        pr, pc, _ = partner(step)
        pl.semaphore_signal(barrier, inc=1, device_id=(pr, pc), device_id_type=MESH)

    pl.semaphore_wait(barrier, n - 1)

    def t_copy(sender, pr, pc, dest):
        return pltpu.make_async_remote_copy(
            src_ref=t_ref.at[:, pl.ds(pl.multiple_of(dest * block, 128), block)],
            dst_ref=tdir.at[pl.ds(pl.multiple_of(sender * own, own), own), :],
            send_sem=t_send.at[dest],
            recv_sem=t_recv.at[sender],
            device_id=(pr, pc),
            device_id_type=MESH,
        )

    @pl.loop(1, n)
    def _(step):
        pr, pc, dest = partner(step)
        t_copy(me, pr, pc, dest).start()

    def w_block(pc):
        return w_ref[pl.ds(pl.multiple_of(pc * block, 128), block), :].T

    def w_copy(sender, dest):
        return pltpu.make_async_remote_copy(
            src_ref=wt.at[dest],
            dst_ref=wr.at[sender],
            send_sem=w_send.at[dest],
            recv_sem=w_recv.at[sender],
            device_id=(r, dest),
            device_id_type=MESH,
        )

    @pl.loop(1, cols)
    def _(step):
        _, pc, _ = partner(step)
        wt[pc] = w_block(pc)
        w_copy(c, pc).start()

    wr[c] = w_block(c)
    tdir[pl.ds(pl.multiple_of(me * own, own), own), :] = t_ref[
        :, pl.ds(pl.multiple_of(me * block, 128), block)
    ]

    @pl.loop(0, n)
    def _(part):
        x = t_ref[:, pl.ds(pl.multiple_of(part * block, 128), block)]
        for j in range(own):
            piece = jnp.pad(x[:, j * O : (j + 1) * O], ((0, 0), (0, 128 - O)))
            for half in range(0, own, 8):
                u[pl.ds(half * count + part * own + j, 8, stride=count), :] = piece[
                    half : half + 8
                ]

    for j in range(own):
        sw[:, j * O : (j + 1) * O] = u[j * count : (j + 1) * count, 0:O]

    def combine(source):
        at = pl.ds(pl.multiple_of(source * own, own), own)
        high, low = halves(2.0 * tdir[at, :] - sw[at, :])
        dh[at, :] = high
        dl[at, :] = low

    combine(me)

    @pl.loop(1, n)
    def _(step):
        pr, pc, source = partner(step)
        t_copy(source, pr, pc, me).wait_recv()
        combine(source)

    def r_copy(pc, sender, dest):
        return pltpu.make_async_remote_copy(
            src_ref=pbuf.at[pc, pl.ds(pl.multiple_of(dest * own, own), own), :],
            dst_ref=rbuf.at[pc, sender],
            send_sem=r_send.at[pc, dest],
            recv_sem=r_recv.at[pc, sender],
            device_id=(dest, c),
            device_id_type=MESH,
        )

    def c_copy(sender, dest):
        return pltpu.make_async_remote_copy(
            src_ref=qbuf.at[dest],
            dst_ref=cbuf.at[sender],
            send_sem=c_send.at[dest],
            recv_sem=c_recv.at[sender],
            device_id=(r, dest),
            device_id_type=MESH,
        )

    def multiply(pc):
        high, low = halves(wr[pc])
        both = dot_nt(jnp.concatenate([high, low], axis=0), dh[...])
        pbuf[pc] = both[:chunk] + both[chunk:] + dot_nt(high, dl[...])
        for i in range(1, rows):
            dest = (r + i) % rows
            r_copy(pc, r, dest).start()

    def collect(pc):
        total = pbuf[pc, pl.ds(pl.multiple_of(r * own, own), own), :]
        for i in range(1, rows):
            sender = (r + i) % rows
            r_copy(pc, sender, r).wait_recv()
            total = total + rbuf[pc, sender]
        qbuf[pc] = total

    multiply(c)

    @pl.loop(1, cols)
    def _(step):
        _, pc, _ = partner(step)
        w_copy(pc, c).wait_recv()
        multiply(pc)
        _, before, _ = partner(step - 1)
        collect(before)

        @pl.when(step > 1)
        def _():
            c_copy(c, before).start()

    _, last, _ = partner(cols - 1)
    collect(last)
    c_copy(c, last).start()

    qt[...] = qbuf[...].reshape(cols * own, count).T

    def m_copy(sender, pr, pc, dest):
        return pltpu.make_async_remote_copy(
            src_ref=qt.at[pl.ds(pl.multiple_of(dest * own, own), own), :],
            dst_ref=mbuf.at[sender],
            send_sem=m_send.at[dest],
            recv_sem=m_recv.at[sender],
            device_id=(pr, pc),
            device_id_type=MESH,
        )

    @pl.loop(1, n)
    def _(step):
        pr, pc, dest = partner(step)
        m_copy(me, pr, pc, dest).start()

    mbuf[me] = qt[pl.ds(pl.multiple_of(me * own, own), own), :]
    cbuf[c] = qbuf[c]

    @pl.loop(1, cols)
    def _(step):
        _, pc, _ = partner(step)
        c_copy(pc, c).wait_recv()

    @pl.loop(1, n)
    def _(step):
        pr, pc, source = partner(step)
        m_copy(source, pr, pc, me).wait_recv()

    mirrored = jnp.sum(cbuf[...], axis=0)
    lanes = cols * own
    for i in range(rows):
        at = slice(i * lanes, (i + 1) * lanes)
        out_ref[:, at] = mirrored[:, at] + jnp.sum(mbuf[i * cols : (i + 1) * cols], axis=0)

    @pl.loop(1, n)
    def _(step):
        pr, pc, dest = partner(step)
        t_copy(me, pr, pc, dest).wait_send()
        m_copy(me, pr, pc, dest).wait_send()

    @pl.loop(1, cols)
    def _(step):
        _, pc, _ = partner(step)
        w_copy(c, pc).wait_send()
        c_copy(c, pc).wait_send()

    @pl.loop(0, cols)
    def _(pc):
        for i in range(1, rows):
            r_copy(pc, r, (r + i) % rows).wait_send()


def in_one_kernel(multiplier, cycle_tiles):
    own, width = multiplier.shape
    rows, cols = lax.axis_size("row"), lax.axis_size("col")
    n = rows * cols
    block, chunk, count = width // n, cycle_tiles.shape[1], own * n
    f32, bf16 = jnp.float32, jnp.bfloat16
    dma = pltpu.SemaphoreType.DMA
    return pl.pallas_call(
        functools.partial(cycle_kernel, rows, cols),
        out_shape=jax.ShapeDtypeStruct((own, count), f32),
        in_specs=[pl.BlockSpec(memory_space=pltpu.VMEM)] * 2,
        out_specs=pl.BlockSpec(memory_space=pltpu.VMEM),
        scratch_shapes=[
            pltpu.VMEM((cols, chunk, block), f32),
            pltpu.VMEM((count, block), f32),
            pltpu.VMEM((own * count, 128), f32),
            pltpu.VMEM((count, block), f32),
            pltpu.VMEM((count, block), bf16),
            pltpu.VMEM((count, block), bf16),
            pltpu.VMEM((cols, chunk, block), f32),
            pltpu.VMEM((cols, chunk, count), f32),
            pltpu.VMEM((cols, rows, own, count), f32),
            pltpu.VMEM((cols, own, count), f32),
            pltpu.VMEM((cols, own, count), f32),
            pltpu.VMEM((count, cols * own), f32),
            pltpu.VMEM((n, own, cols * own), f32),
            dma((n,)), dma((n,)), dma((cols,)), dma((cols,)),
            dma((cols, rows)), dma((cols, rows)),
            dma((cols,)), dma((cols,)), dma((n,)), dma((n,)),
        ],
        compiler_params=pltpu.CompilerParams(
            collective_id=0, has_side_effects=True, vmem_limit_bytes=48 * 1024 * 1024
        ),
        cost_estimate=pl.CostEstimate(
            flops=6 * count * block * count, bytes_accessed=4 * own * width, transcendentals=0
        ),
    )(multiplier, cycle_tiles)


def in_collectives(multiplier, cycle_tiles):
    rows_loc, full_width = multiplier.shape
    row_count = lax.axis_size("row")
    col_count = lax.axis_size("col")
    devices = row_count * col_count
    block_width = full_width // devices
    out_block = cycle_tiles.shape[1] // row_count
    virt_dev = rows_loc // OW
    all_rows = rows_loc * devices
    pieces = multiplier.reshape(1, rows_loc, devices, block_width)
    moved = lax.all_to_all(pieces, ("row", "col"), split_axis=2, concat_axis=0, tiled=True)
    direct = moved.reshape(all_rows, block_width)
    cycle_rows = lax.all_to_all(cycle_tiles.T, "col", split_axis=1, concat_axis=0, tiled=True)
    swapped = jnp.transpose(multiplier.reshape(virt_dev, OW, V, O), (2, 1, 0, 3)).reshape(
        all_rows, block_width
    )
    combined = 2.0 * direct - swapped
    partial_value = lax.dot_general(
        cycle_rows,
        combined,
        (((1,), (1,)), ((), ())),
        precision=lax.Precision.HIGHEST,
        preferred_element_type=jnp.float32,
    )
    partial_value = partial_value.reshape(col_count, row_count, out_block, all_rows)
    over_row = lax.psum_scatter(partial_value, "row", scatter_dimension=1, tiled=True)
    own_cols = lax.psum_scatter(over_row, "col", scatter_dimension=0, tiled=True)
    own_cols = own_cols.reshape(out_block, all_rows)
    outgoing = own_cols.reshape(1, out_block, devices, rows_loc)
    arrived = lax.all_to_all(outgoing, ("row", "col"), split_axis=2, concat_axis=0, tiled=True)
    own_rows = arrived.reshape(devices * out_block, rows_loc).T
    return own_rows + own_cols


def on_device(multiplier, cycle_tiles):
    own, width = multiplier.shape
    rows, cols = lax.axis_size("row"), lax.axis_size("col")
    block = width // (rows * cols)
    powers = rows & (rows - 1) == 0 and cols & (cols - 1) == 0
    whole_tiles = own % 16 == 0 and block % 128 == 0 and (cols * own) % 128 == 0
    if OW == 1 and O <= 128 and powers and whole_tiles and block == own * O:
        return in_one_kernel(multiplier, cycle_tiles)
    return in_collectives(multiplier, cycle_tiles)


def solution(mesh):
    placed = (P(("row", "col"), None), P("row", "col"))
    return jax.shard_map(
        on_device, mesh=mesh, in_specs=placed, out_specs=P(("row", "col"), None), check_vma=False
    )
```

```python
import functools

import jax
import jax.numpy as jnp
from jax import lax
from jax.experimental import pallas as pl
from jax.experimental.pallas import tpu as pltpu
from jax.sharding import PartitionSpec as P

O = 40
V = 512
OW = 1
MESH = pl.DeviceIdType.MESH


def flip(x, y, size):
    total, bit = 0, 1
    while bit < size:
        total = total + bit * ((x // bit + y // bit) % 2)
        bit *= 2
    return total


def halves(x):
    high = x.astype(jnp.bfloat16)
    return high, (x - high.astype(jnp.float32)).astype(jnp.bfloat16)


def dot_nt(x, y):
    return lax.dot_general(
        x, y, (((1,), (1,)), ((), ())), preferred_element_type=jnp.float32
    )


def cycle_kernel(
    rows, cols, t_hbm, w_hbm, out_ref,
    t_ref, tdir, u, sw, dh, dl, wr, pbuf, rbuf, qbuf, cbuf, tall, fbuf, fr, flat,
    here, t_send, t_recv, w_send, w_recv, r_send, r_recv, c_send, c_recv, f_send, f_recv,
):
    n = rows * cols
    own, width = t_ref.shape
    block = width // n
    chunk = w_hbm.shape[0]
    count = own * n
    r = lax.axis_index("row")
    c = lax.axis_index("col")
    me = r * cols + c

    core = c % 2
    t_here = pltpu.make_async_copy(t_hbm, t_ref, here.at[0])
    t_here.start()
    w_here = pltpu.make_async_copy(
        w_hbm.at[:, pl.ds(pl.multiple_of(c * block, 128), block)], wr.at[c], here.at[1]
    )
    w_here.start()

    def mask_of(step):
        s = step % cols
        return (s % 2) * (cols // 2) + s // 2

    def partner(step):
        s, q = step % cols, step // cols
        pr = flip(r, (q + s) % rows, rows)
        pc = flip(c, mask_of(step), cols)
        return pr, pc, pr * cols + pc

    barrier = pltpu.get_barrier_semaphore()

    @pl.loop(1, n)
    def _(step):
        pr, pc, _ = partner(step)
        pl.semaphore_signal(barrier, inc=1, device_id=(pr, pc), device_id_type=MESH)

    pl.semaphore_wait(barrier, n - 1)

    def t_copy(sender, pr, pc, dest):
        return pltpu.make_async_remote_copy(
            src_ref=t_hbm.at[:, pl.ds(pl.multiple_of(dest * block, 128), block)],
            dst_ref=tdir.at[pl.ds(pl.multiple_of(sender * own, own), own), :],
            send_sem=t_send.at[dest],
            recv_sem=t_recv.at[sender],
            device_id=(pr, pc),
            device_id_type=MESH,
        )

    @pl.loop(1, n)
    def _(step):
        pr, pc, dest = partner(step)
        t_copy(me, pr, pc, dest).start()

    def w_copy(sender, dest):
        return pltpu.make_async_remote_copy(
            src_ref=w_hbm.at[:, pl.ds(pl.multiple_of(dest * block, 128), block)],
            dst_ref=wr.at[sender],
            send_sem=w_send.at[dest],
            recv_sem=w_recv.at[sender],
            device_id=(r, dest),
            device_id_type=MESH,
        )

    @pl.loop(1, cols)
    def _(step):
        _, pc, _ = partner(step)
        w_copy(c, pc).start()

    t_here.wait()
    tdir[pl.ds(pl.multiple_of(me * own, own), own), :] = t_ref[
        :, pl.ds(pl.multiple_of(me * block, 128), block)
    ]

    @pl.loop(0, n)
    def _(part):
        x = t_ref[:, pl.ds(pl.multiple_of(part * block, 128), block)]
        for j in range(own):
            piece = jnp.pad(x[:, j * O : (j + 1) * O], ((0, 0), (0, 128 - O)))
            for half in range(0, own, 8):
                u[pl.ds(half * count + part * own + j, 8, stride=count), :] = piece[
                    half : half + 8
                ]

    for j in range(own):
        sw[:, j * O : (j + 1) * O] = u[j * count : (j + 1) * count, 0:O]

    def combine(source):
        at = pl.ds(pl.multiple_of(source * own, own), own)
        high, low = halves(2.0 * tdir[at, :] - sw[at, :])
        dh[at, :] = high
        dl[at, :] = low

    combine(me)

    @pl.loop(1, n)
    def _(step):
        pr, pc, source = partner(step)
        t_copy(source, pr, pc, me).wait_recv()
        combine(source)

    def r_copy(pc, sender_row, sender_core, dest):
        return pltpu.make_async_remote_copy(
            src_ref=pbuf.at[pc, pl.ds(pl.multiple_of(dest * own, own), own), :],
            dst_ref=rbuf.at[pc // 2, sender_row, sender_core],
            send_sem=r_send.at[pc, dest],
            recv_sem=r_recv.at[pc // 2, sender_row, sender_core],
            device_id=(dest, c - core + pc % 2),
            device_id_type=MESH,
        )

    def c_copy(sender, dest):
        return pltpu.make_async_remote_copy(
            src_ref=qbuf.at[dest // 2],
            dst_ref=cbuf.at[sender // 2],
            send_sem=c_send.at[dest // 2],
            recv_sem=c_recv.at[sender // 2],
            device_id=(r, dest),
            device_id_type=MESH,
        )

    def multiply(pc):
        high, low = halves(wr[pc])
        both = dot_nt(jnp.concatenate([high, low], axis=0), dh[...])
        pbuf[pc] = both[:chunk] + both[chunk:] + dot_nt(high, dl[...])
        for i in range(1, rows):
            r_copy(pc, r, core, (r + i) % rows).start()

        @pl.when(pc % 2 != core)
        def _():
            r_copy(pc, r, core, r).start()

    def collect(pc):
        total = pbuf[pc, pl.ds(pl.multiple_of(r * own, own), own), :]
        for i in range(rows):
            for k in range(2):
                if i or k:
                    sender, side = (r + i) % rows, (core + k) % 2
                    r_copy(pc, sender, side, r).wait_recv()
                    total = total + rbuf[pc // 2, sender, side]
        qbuf[pc // 2] = total

    steps = [mask_of(step) for step in range(cols)]
    ready = {m: max(steps.index(m), steps.index(m + 1)) + 1 for m in range(0, cols, 2)}
    order = sorted(ready, key=lambda m: ready[m])

    def collect_mask(mask):
        pc = flip(c, mask, cols)
        collect(pc)
        if mask:
            c_copy(c, pc).start()

    w_here.wait()
    multiply(c)

    @pl.loop(1, cols)
    def _(step):
        _, pc, _ = partner(step)
        w_copy(pc, c).wait_recv()
        multiply(pc)
        for mask in order:
            if ready[mask] < cols:
                pl.when(step == ready[mask])(functools.partial(collect_mask, mask))

    for mask in order:
        if ready[mask] >= cols:
            collect_mask(mask)

    full = qbuf[c // 2]
    for mask in order:
        if mask:
            pc = flip(c, mask, cols)
            c_copy(pc, c).wait_recv()
            full = full + cbuf[pc // 2]

    per = 128 // own
    parts = own // per
    tall[...] = jnp.pad(full.T, ((0, 0), (0, 128 - own)))
    packed = jnp.concatenate(
        [tall[pl.ds(j, n * parts, stride=per), :][:, :own] for j in range(per)], axis=1
    )
    for d in range(n):
        fbuf[d] = packed[d * parts : (d + 1) * parts]

    def f_copy(sender, pr, pc, dest):
        return pltpu.make_async_remote_copy(
            src_ref=fbuf.at[dest],
            dst_ref=fr.at[sender],
            send_sem=f_send.at[dest],
            recv_sem=f_recv.at[sender],
            device_id=(pr, pc),
            device_id_type=MESH,
        )

    @pl.loop(1, n)
    def _(step):
        pr, pc, dest = partner(step)
        f_copy(me, pr, pc, dest).start()

    fr[me] = fbuf[me]

    @pl.loop(1, n)
    def _(step):
        pr, pc, dest = partner(step)
        t_copy(me, pr, pc, dest).wait_send()

    @pl.loop(1, cols)
    def _(step):
        _, pc, _ = partner(step)
        w_copy(c, pc).wait_send()

    for mask in order:
        if mask:
            c_copy(c, flip(c, mask, cols)).wait_send()

    @pl.loop(0, cols)
    def _(pc):
        for i in range(1, rows):
            r_copy(pc, r, core, (r + i) % rows).wait_send()

        @pl.when(pc % 2 != core)
        def _():
            r_copy(pc, r, core, r).wait_send()

    @pl.loop(1, n)
    def _(step):
        pr, pc, source = partner(step)
        f_copy(source, pr, pc, me).wait_recv()

    for d in range(n):
        flat[d * parts : (d + 1) * parts, :] = fr[d]
    got = flat[...]
    for j in range(per):
        tall[pl.ds(j, n * parts, stride=per), :] = jnp.pad(
            got[:, j * own : (j + 1) * own], ((0, 0), (0, 128 - own))
        )
    across = jnp.concatenate([tall[d * own : (d + 1) * own, :own] for d in range(n)], axis=1)
    out_ref[...] = full + across

    @pl.loop(1, n)
    def _(step):
        pr, pc, dest = partner(step)
        f_copy(me, pr, pc, dest).wait_send()


def in_one_kernel(multiplier, cycle_tiles):
    own, width = multiplier.shape
    rows, cols = lax.axis_size("row"), lax.axis_size("col")
    n = rows * cols
    block, chunk, count = width // n, cycle_tiles.shape[1], own * n
    parts = own * own // 128
    f32, bf16 = jnp.float32, jnp.bfloat16
    dma = pltpu.SemaphoreType.DMA
    return pl.pallas_call(
        functools.partial(cycle_kernel, rows, cols),
        out_shape=jax.ShapeDtypeStruct((own, count), f32),
        in_specs=[pl.BlockSpec(memory_space=pltpu.HBM)] * 2,
        out_specs=pl.BlockSpec(memory_space=pltpu.VMEM),
        scratch_shapes=[
            pltpu.VMEM((own, width), f32),
            pltpu.VMEM((count, block), f32),
            pltpu.VMEM((own * count, 128), f32),
            pltpu.VMEM((count, block), f32),
            pltpu.VMEM((count, block), bf16),
            pltpu.VMEM((count, block), bf16),
            pltpu.VMEM((cols, chunk, block), f32),
            pltpu.VMEM((cols, chunk, count), f32),
            pltpu.VMEM((cols // 2, rows, 2, own, count), f32),
            pltpu.VMEM((cols // 2, own, count), f32),
            pltpu.VMEM((cols // 2, own, count), f32),
            pltpu.VMEM((count, 128), f32),
            pltpu.VMEM((n, parts, 128), f32),
            pltpu.VMEM((n, parts, 128), f32),
            pltpu.VMEM((n * parts, 128), f32),
            dma((2,)), dma((n,)), dma((n,)), dma((cols,)), dma((cols,)),
            dma((cols, rows)), dma((cols // 2, rows, 2)),
            dma((cols // 2,)), dma((cols // 2,)), dma((n,)), dma((n,)),
        ],
        compiler_params=pltpu.CompilerParams(
            collective_id=0, has_side_effects=True, vmem_limit_bytes=62 * 1024 * 1024
        ),
        cost_estimate=pl.CostEstimate(
            flops=6 * count * block * count, bytes_accessed=4 * own * width, transcendentals=0
        ),
    )(multiplier, cycle_tiles.T)


def in_collectives(multiplier, cycle_tiles):
    rows_loc, full_width = multiplier.shape
    row_count = lax.axis_size("row")
    col_count = lax.axis_size("col")
    devices = row_count * col_count
    block_width = full_width // devices
    out_block = cycle_tiles.shape[1] // row_count
    virt_dev = rows_loc // OW
    all_rows = rows_loc * devices
    pieces = multiplier.reshape(1, rows_loc, devices, block_width)
    moved = lax.all_to_all(pieces, ("row", "col"), split_axis=2, concat_axis=0, tiled=True)
    direct = moved.reshape(all_rows, block_width)
    cycle_rows = lax.all_to_all(cycle_tiles.T, "col", split_axis=1, concat_axis=0, tiled=True)
    swapped = jnp.transpose(multiplier.reshape(virt_dev, OW, V, O), (2, 1, 0, 3)).reshape(
        all_rows, block_width
    )
    combined = 2.0 * direct - swapped
    partial_value = lax.dot_general(
        cycle_rows,
        combined,
        (((1,), (1,)), ((), ())),
        precision=lax.Precision.HIGHEST,
        preferred_element_type=jnp.float32,
    )
    partial_value = partial_value.reshape(col_count, row_count, out_block, all_rows)
    over_row = lax.psum_scatter(partial_value, "row", scatter_dimension=1, tiled=True)
    own_cols = lax.psum_scatter(over_row, "col", scatter_dimension=0, tiled=True)
    own_cols = own_cols.reshape(out_block, all_rows)
    outgoing = own_cols.reshape(1, out_block, devices, rows_loc)
    arrived = lax.all_to_all(outgoing, ("row", "col"), split_axis=2, concat_axis=0, tiled=True)
    own_rows = arrived.reshape(devices * out_block, rows_loc).T
    return own_rows + own_cols


def on_device(multiplier, cycle_tiles):
    own, width = multiplier.shape
    rows, cols = lax.axis_size("row"), lax.axis_size("col")
    block = width // (rows * cols)
    powers = rows & (rows - 1) == 0 and cols & (cols - 1) == 0
    whole_tiles = own % 16 == 0 and 128 % own == 0 and block % 128 == 0 and cols > 1
    if OW == 1 and O <= 128 and powers and whole_tiles and block == own * O:
        return in_one_kernel(multiplier, cycle_tiles)
    return in_collectives(multiplier, cycle_tiles)


def solution(mesh):
    placed = (P(("row", "col"), None), P("row", "col"))
    return jax.shard_map(
        on_device, mesh=mesh, in_specs=placed, out_specs=P(("row", "col"), None), check_vma=False
    )
```

```python
import functools

import jax
import jax.numpy as jnp
from jax import lax
from jax.experimental import pallas as pl
from jax.experimental.pallas import tpu as pltpu
from jax.sharding import PartitionSpec as P

O = 40
V = 512
OW = 1
MESH = pl.DeviceIdType.MESH


def flip(x, y, size):
    total, bit = 0, 1
    while bit < size:
        total = total + bit * ((x // bit + y // bit) % 2)
        bit *= 2
    return total


def halves(x):
    high = x.astype(jnp.bfloat16)
    return high, (x - high.astype(jnp.float32)).astype(jnp.bfloat16)


def dot_nt(x, y):
    return lax.dot_general(
        x, y, (((1,), (1,)), ((), ())), preferred_element_type=jnp.float32
    )


def cycle_kernel(
    rows, cols, t_hbm, w_hbm, out_ref,
    t_ref, tdir, u, sw, dh, dl, wr, pbuf, rbuf, qbuf, cbuf, tall, fbuf, fr, flat,
    here, t_send, t_recv, w_send, w_recv, r_send, r_recv, c_send, c_recv, f_send, f_recv,
):
    n = rows * cols
    own, width = t_ref.shape
    block = width // n
    chunk = w_hbm.shape[0]
    count = own * n
    r = lax.axis_index("row")
    c = lax.axis_index("col")
    me = r * cols + c

    core = c % 2
    t_here = pltpu.make_async_copy(t_hbm, t_ref, here.at[0])
    t_here.start()
    w_here = pltpu.make_async_copy(
        w_hbm.at[:, pl.ds(pl.multiple_of(c * block, 128), block)], wr.at[c], here.at[1]
    )
    w_here.start()

    def mask_of(step):
        s = step % cols
        return (s % 2) * (cols // 2) + s // 2

    def partner(step):
        s, q = step % cols, step // cols
        pr = flip(r, (q + s) % rows, rows)
        pc = flip(c, mask_of(step), cols)
        return pr, pc, pr * cols + pc

    barrier = pltpu.get_barrier_semaphore()

    @pl.loop(1, n)
    def _(step):
        pr, pc, _ = partner(step)
        pl.semaphore_signal(barrier, inc=1, device_id=(pr, pc), device_id_type=MESH)

    pl.semaphore_wait(barrier, n - 1)

    def t_copy(sender, pr, pc, dest):
        return pltpu.make_async_remote_copy(
            src_ref=t_hbm.at[:, pl.ds(pl.multiple_of(dest * block, 128), block)],
            dst_ref=tdir.at[pl.ds(pl.multiple_of(sender * own, own), own), :],
            send_sem=t_send.at[dest],
            recv_sem=t_recv.at[sender],
            device_id=(pr, pc),
            device_id_type=MESH,
        )

    @pl.loop(1, n)
    def _(step):
        pr, pc, dest = partner(step)
        t_copy(me, pr, pc, dest).start()

    def w_copy(sender, dest):
        return pltpu.make_async_remote_copy(
            src_ref=w_hbm.at[:, pl.ds(pl.multiple_of(dest * block, 128), block)],
            dst_ref=wr.at[sender],
            send_sem=w_send.at[dest],
            recv_sem=w_recv.at[sender],
            device_id=(r, dest),
            device_id_type=MESH,
        )

    t_here.wait()
    tdir[pl.ds(pl.multiple_of(me * own, own), own), :] = t_ref[
        :, pl.ds(pl.multiple_of(me * block, 128), block)
    ]

    @pl.loop(0, n)
    def _(part):
        x = t_ref[:, pl.ds(pl.multiple_of(part * block, 128), block)]
        for j in range(own):
            piece = jnp.pad(x[:, j * O : (j + 1) * O], ((0, 0), (0, 128 - O)))
            for half in range(0, own, 8):
                u[pl.ds(half * count + part * own + j, 8, stride=count), :] = piece[
                    half : half + 8
                ]

    for j in range(own):
        sw[:, j * O : (j + 1) * O] = u[j * count : (j + 1) * count, 0:O]

    def combine(source):
        at = pl.ds(pl.multiple_of(source * own, own), own)
        high, low = halves(2.0 * tdir[at, :] - sw[at, :])
        dh[at, :] = high
        dl[at, :] = low

    left = n - n // 8

    @pl.loop(1, left)
    def _(step):
        pr, pc, dest = partner(step)
        t_copy(me, pr, pc, dest).wait_send()

    @pl.loop(1, cols)
    def _(step):
        _, pc, _ = partner(step)
        w_copy(c, pc).start()

    combine(me)

    @pl.loop(1, n)
    def _(step):
        pr, pc, source = partner(step)
        t_copy(source, pr, pc, me).wait_recv()
        combine(source)

    def r_copy(pc, sender_row, sender_core, dest):
        return pltpu.make_async_remote_copy(
            src_ref=pbuf.at[pc, pl.ds(pl.multiple_of(dest * own, own), own), :],
            dst_ref=rbuf.at[pc // 2, sender_row, sender_core],
            send_sem=r_send.at[pc, dest],
            recv_sem=r_recv.at[pc // 2, sender_row, sender_core],
            device_id=(dest, c - core + pc % 2),
            device_id_type=MESH,
        )

    def c_copy(sender, dest):
        return pltpu.make_async_remote_copy(
            src_ref=qbuf.at[dest // 2],
            dst_ref=cbuf.at[sender // 2],
            send_sem=c_send.at[dest // 2],
            recv_sem=c_recv.at[sender // 2],
            device_id=(r, dest),
            device_id_type=MESH,
        )

    def multiply(pc):
        high, low = halves(wr[pc])
        both = dot_nt(jnp.concatenate([high, low], axis=0), dh[...])
        pbuf[pc] = both[:chunk] + both[chunk:] + dot_nt(high, dl[...])
        for i in range(1, rows):
            r_copy(pc, r, core, (r + i) % rows).start()

        @pl.when(pc % 2 != core)
        def _():
            r_copy(pc, r, core, r).start()

    def collect(pc):
        total = pbuf[pc, pl.ds(pl.multiple_of(r * own, own), own), :]
        for i in range(rows):
            for k in range(2):
                if i or k:
                    sender, side = (r + i) % rows, (core + k) % 2
                    r_copy(pc, sender, side, r).wait_recv()
                    total = total + rbuf[pc // 2, sender, side]
        qbuf[pc // 2] = total

    steps = [mask_of(step) for step in range(cols)]
    ready = {m: max(steps.index(m), steps.index(m + 1)) + 1 for m in range(0, cols, 2)}
    order = sorted(ready, key=lambda m: ready[m])

    def collect_mask(mask):
        pc = flip(c, mask, cols)
        collect(pc)
        if mask:
            c_copy(c, pc).start()

    w_here.wait()
    multiply(c)

    @pl.loop(1, cols)
    def _(step):
        _, pc, _ = partner(step)
        w_copy(pc, c).wait_recv()
        multiply(pc)
        for mask in order:
            if ready[mask] < cols:
                pl.when(step == ready[mask])(functools.partial(collect_mask, mask))

    for mask in order:
        if ready[mask] >= cols:
            collect_mask(mask)

    full = qbuf[c // 2]
    for mask in order:
        if mask:
            pc = flip(c, mask, cols)
            c_copy(pc, c).wait_recv()
            full = full + cbuf[pc // 2]

    per = 128 // own
    parts = own // per
    tall[...] = jnp.pad(full.T, ((0, 0), (0, 128 - own)))
    packed = jnp.concatenate(
        [tall[pl.ds(j, n * parts, stride=per), :][:, :own] for j in range(per)], axis=1
    )
    for d in range(n):
        fbuf[d] = packed[d * parts : (d + 1) * parts]

    def f_copy(sender, pr, pc, dest):
        return pltpu.make_async_remote_copy(
            src_ref=fbuf.at[dest],
            dst_ref=fr.at[sender],
            send_sem=f_send.at[dest],
            recv_sem=f_recv.at[sender],
            device_id=(pr, pc),
            device_id_type=MESH,
        )

    @pl.loop(1, n)
    def _(step):
        pr, pc, dest = partner(step)
        f_copy(me, pr, pc, dest).start()

    fr[me] = fbuf[me]

    @pl.loop(left, n)
    def _(step):
        pr, pc, dest = partner(step)
        t_copy(me, pr, pc, dest).wait_send()

    @pl.loop(1, cols)
    def _(step):
        _, pc, _ = partner(step)
        w_copy(c, pc).wait_send()

    for mask in order:
        if mask:
            c_copy(c, flip(c, mask, cols)).wait_send()

    @pl.loop(0, cols)
    def _(pc):
        for i in range(1, rows):
            r_copy(pc, r, core, (r + i) % rows).wait_send()

        @pl.when(pc % 2 != core)
        def _():
            r_copy(pc, r, core, r).wait_send()

    @pl.loop(1, n)
    def _(step):
        pr, pc, source = partner(step)
        f_copy(source, pr, pc, me).wait_recv()

    for d in range(n):
        flat[d * parts : (d + 1) * parts, :] = fr[d]
    got = flat[...]
    for j in range(per):
        tall[pl.ds(j, n * parts, stride=per), :] = jnp.pad(
            got[:, j * own : (j + 1) * own], ((0, 0), (0, 128 - own))
        )
    across = jnp.concatenate([tall[d * own : (d + 1) * own, :own] for d in range(n)], axis=1)
    out_ref[...] = full + across

    @pl.loop(1, n)
    def _(step):
        pr, pc, dest = partner(step)
        f_copy(me, pr, pc, dest).wait_send()


def in_one_kernel(multiplier, cycle_tiles):
    own, width = multiplier.shape
    rows, cols = lax.axis_size("row"), lax.axis_size("col")
    n = rows * cols
    block, chunk, count = width // n, cycle_tiles.shape[1], own * n
    parts = own * own // 128
    f32, bf16 = jnp.float32, jnp.bfloat16
    dma = pltpu.SemaphoreType.DMA
    return pl.pallas_call(
        functools.partial(cycle_kernel, rows, cols),
        out_shape=jax.ShapeDtypeStruct((own, count), f32),
        in_specs=[pl.BlockSpec(memory_space=pltpu.HBM)] * 2,
        out_specs=pl.BlockSpec(memory_space=pltpu.VMEM),
        scratch_shapes=[
            pltpu.VMEM((own, width), f32),
            pltpu.VMEM((count, block), f32),
            pltpu.VMEM((own * count, 128), f32),
            pltpu.VMEM((count, block), f32),
            pltpu.VMEM((count, block), bf16),
            pltpu.VMEM((count, block), bf16),
            pltpu.VMEM((cols, chunk, block), f32),
            pltpu.VMEM((cols, chunk, count), f32),
            pltpu.VMEM((cols // 2, rows, 2, own, count), f32),
            pltpu.VMEM((cols // 2, own, count), f32),
            pltpu.VMEM((cols // 2, own, count), f32),
            pltpu.VMEM((count, 128), f32),
            pltpu.VMEM((n, parts, 128), f32),
            pltpu.VMEM((n, parts, 128), f32),
            pltpu.VMEM((n * parts, 128), f32),
            dma((2,)), dma((n,)), dma((n,)), dma((cols,)), dma((cols,)),
            dma((cols, rows)), dma((cols // 2, rows, 2)),
            dma((cols // 2,)), dma((cols // 2,)), dma((n,)), dma((n,)),
        ],
        compiler_params=pltpu.CompilerParams(
            collective_id=0, has_side_effects=True, vmem_limit_bytes=62 * 1024 * 1024
        ),
        cost_estimate=pl.CostEstimate(
            flops=6 * count * block * count, bytes_accessed=4 * own * width, transcendentals=0
        ),
    )(multiplier, cycle_tiles.T)


def in_collectives(multiplier, cycle_tiles):
    rows_loc, full_width = multiplier.shape
    row_count = lax.axis_size("row")
    col_count = lax.axis_size("col")
    devices = row_count * col_count
    block_width = full_width // devices
    out_block = cycle_tiles.shape[1] // row_count
    virt_dev = rows_loc // OW
    all_rows = rows_loc * devices
    pieces = multiplier.reshape(1, rows_loc, devices, block_width)
    moved = lax.all_to_all(pieces, ("row", "col"), split_axis=2, concat_axis=0, tiled=True)
    direct = moved.reshape(all_rows, block_width)
    cycle_rows = lax.all_to_all(cycle_tiles.T, "col", split_axis=1, concat_axis=0, tiled=True)
    swapped = jnp.transpose(multiplier.reshape(virt_dev, OW, V, O), (2, 1, 0, 3)).reshape(
        all_rows, block_width
    )
    combined = 2.0 * direct - swapped
    partial_value = lax.dot_general(
        cycle_rows,
        combined,
        (((1,), (1,)), ((), ())),
        precision=lax.Precision.HIGHEST,
        preferred_element_type=jnp.float32,
    )
    partial_value = partial_value.reshape(col_count, row_count, out_block, all_rows)
    over_row = lax.psum_scatter(partial_value, "row", scatter_dimension=1, tiled=True)
    own_cols = lax.psum_scatter(over_row, "col", scatter_dimension=0, tiled=True)
    own_cols = own_cols.reshape(out_block, all_rows)
    outgoing = own_cols.reshape(1, out_block, devices, rows_loc)
    arrived = lax.all_to_all(outgoing, ("row", "col"), split_axis=2, concat_axis=0, tiled=True)
    own_rows = arrived.reshape(devices * out_block, rows_loc).T
    return own_rows + own_cols


def on_device(multiplier, cycle_tiles):
    own, width = multiplier.shape
    rows, cols = lax.axis_size("row"), lax.axis_size("col")
    block = width // (rows * cols)
    powers = rows & (rows - 1) == 0 and cols & (cols - 1) == 0
    whole_tiles = own % 16 == 0 and 128 % own == 0 and block % 128 == 0 and cols > 1
    if OW == 1 and O <= 128 and powers and whole_tiles and block == own * O:
        return in_one_kernel(multiplier, cycle_tiles)
    return in_collectives(multiplier, cycle_tiles)


def solution(mesh):
    placed = (P(("row", "col"), None), P("row", "col"))
    return jax.shard_map(
        on_device, mesh=mesh, in_specs=placed, out_specs=P(("row", "col"), None), check_vma=False
    )
```

```python
import functools

import jax
import jax.numpy as jnp
from jax import lax
from jax.experimental import pallas as pl
from jax.experimental.pallas import tpu as pltpu
from jax.sharding import PartitionSpec as P

O = 40
V = 512
OW = 1
MESH = pl.DeviceIdType.MESH


def flip(x, y, size):
    total, bit = 0, 1
    while bit < size:
        total = total + bit * ((x // bit + y // bit) % 2)
        bit *= 2
    return total


def halves(x):
    high = x.astype(jnp.bfloat16)
    return high, (x - high.astype(jnp.float32)).astype(jnp.bfloat16)


def dot(x, y):
    return jnp.dot(x, y, preferred_element_type=jnp.float32)


def cycle_kernel(
    rows, cols, t_hbm, w_hbm, out_ref,
    t_ref, tdir, u, sw, dh, dl, wr, pbuf, rbuf, qbuf, cbuf, tall, fbuf, fr, flat,
    here, t_send, t_recv, w_send, w_recv, r_send, r_recv, c_send, c_recv, f_send, f_recv,
):
    n = rows * cols
    own, width = t_ref.shape
    block = width // n
    chunk = w_hbm.shape[0]
    count = own * n
    r = lax.axis_index("row")
    c = lax.axis_index("col")
    me = r * cols + c

    core = c % 2
    t_here = pltpu.make_async_copy(t_hbm, t_ref, here.at[0])
    t_here.start()
    w_here = pltpu.make_async_copy(
        w_hbm.at[:, pl.ds(pl.multiple_of(c * block, 128), block)], wr.at[c], here.at[1]
    )
    w_here.start()

    def mask_of(step):
        s = step % cols
        return (s % 2) * (cols // 2) + s // 2

    def partner(step):
        s, q = step % cols, step // cols
        pr = flip(r, (q + s) % rows, rows)
        pc = flip(c, mask_of(step), cols)
        return pr, pc, pr * cols + pc

    barrier = pltpu.get_barrier_semaphore()

    @pl.loop(1, n)
    def _(step):
        pr, pc, _ = partner(step)
        pl.semaphore_signal(barrier, inc=1, device_id=(pr, pc), device_id_type=MESH)

    pl.semaphore_wait(barrier, n - 1)

    def t_copy(sender, pr, pc, dest):
        return pltpu.make_async_remote_copy(
            src_ref=t_hbm.at[:, pl.ds(pl.multiple_of(dest * block, 128), block)],
            dst_ref=tdir.at[pl.ds(pl.multiple_of(sender * own, own), own), :],
            send_sem=t_send.at[dest],
            recv_sem=t_recv.at[sender],
            device_id=(pr, pc),
            device_id_type=MESH,
        )

    @pl.loop(1, n)
    def _(step):
        pr, pc, dest = partner(step)
        t_copy(me, pr, pc, dest).start()

    def w_copy(sender, dest):
        return pltpu.make_async_remote_copy(
            src_ref=w_hbm.at[:, pl.ds(pl.multiple_of(dest * block, 128), block)],
            dst_ref=wr.at[sender],
            send_sem=w_send.at[dest],
            recv_sem=w_recv.at[sender],
            device_id=(r, dest),
            device_id_type=MESH,
        )

    t_here.wait()
    tdir[pl.ds(pl.multiple_of(me * own, own), own), :] = t_ref[
        :, pl.ds(pl.multiple_of(me * block, 128), block)
    ]

    @pl.loop(0, n)
    def _(part):
        x = t_ref[:, pl.ds(pl.multiple_of(part * block, 128), block)]
        for j in range(own):
            piece = jnp.pad(x[:, j * O : (j + 1) * O], ((0, 0), (0, 128 - O)))
            for half in range(0, own, 8):
                u[pl.ds(half * count + part * own + j, 8, stride=count), :] = piece[
                    half : half + 8
                ]

    for j in range(own):
        sw[:, j * O : (j + 1) * O] = u[j * count : (j + 1) * count, 0:O]

    def combine(source):
        at = pl.ds(pl.multiple_of(source * own, own), own)
        high, low = halves(2.0 * tdir[at, :] - sw[at, :])
        dh[at, :] = high
        dl[at, :] = low

    left = n - n // 8

    @pl.loop(1, left)
    def _(step):
        pr, pc, dest = partner(step)
        t_copy(me, pr, pc, dest).wait_send()

    @pl.loop(1, cols)
    def _(step):
        _, pc, _ = partner(step)
        w_copy(c, pc).start()

    combine(me)

    @pl.loop(1, n)
    def _(step):
        pr, pc, source = partner(step)
        t_copy(source, pr, pc, me).wait_recv()
        combine(source)

    def r_copy(pc, sender_row, sender_core, dest):
        return pltpu.make_async_remote_copy(
            src_ref=pbuf.at[pc, pl.ds(pl.multiple_of(dest * own, own), own), :],
            dst_ref=rbuf.at[pc // 2, sender_row, sender_core],
            send_sem=r_send.at[pc, dest],
            recv_sem=r_recv.at[pc // 2, sender_row, sender_core],
            device_id=(dest, c - core + pc % 2),
            device_id_type=MESH,
        )

    def c_copy(sender, dest):
        return pltpu.make_async_remote_copy(
            src_ref=qbuf.at[dest // 2],
            dst_ref=cbuf.at[sender // 2],
            send_sem=c_send.at[dest // 2],
            recv_sem=c_recv.at[sender // 2],
            device_id=(r, dest),
            device_id_type=MESH,
        )

    def multiply(pc):
        w = wr[pc]
        high = w.astype(jnp.bfloat16).astype(jnp.float32)
        split = jnp.concatenate([high, w - high], axis=0).T.astype(jnp.bfloat16)
        both = (dot(dh[...], split) + dot(dl[...], split)).T
        pbuf[pc] = both[:chunk] + both[chunk:]
        for i in range(1, rows):
            r_copy(pc, r, core, (r + i) % rows).start()

        @pl.when(pc % 2 != core)
        def _():
            r_copy(pc, r, core, r).start()

    def collect(pc):
        total = pbuf[pc, pl.ds(pl.multiple_of(r * own, own), own), :]
        for i in range(rows):
            for k in range(2):
                if i or k:
                    sender, side = (r + i) % rows, (core + k) % 2
                    r_copy(pc, sender, side, r).wait_recv()
                    total = total + rbuf[pc // 2, sender, side]
        qbuf[pc // 2] = total

    steps = [mask_of(step) for step in range(cols)]
    ready = {m: max(steps.index(m), steps.index(m + 1)) + 1 for m in range(0, cols, 2)}
    order = sorted(ready, key=lambda m: ready[m])

    def collect_mask(mask):
        pc = flip(c, mask, cols)
        collect(pc)
        if mask:
            c_copy(c, pc).start()

    w_here.wait()
    multiply(c)

    @pl.loop(1, cols)
    def _(step):
        _, pc, _ = partner(step)
        w_copy(pc, c).wait_recv()
        multiply(pc)
        for mask in order:
            if ready[mask] < cols:
                pl.when(step == ready[mask])(functools.partial(collect_mask, mask))

    for mask in order:
        if ready[mask] >= cols:
            collect_mask(mask)

    full = qbuf[c // 2]
    for mask in order:
        if mask:
            pc = flip(c, mask, cols)
            c_copy(pc, c).wait_recv()
            full = full + cbuf[pc // 2]

    per = 128 // own
    parts = own // per
    tall[...] = jnp.pad(full.T, ((0, 0), (0, 128 - own)))
    packed = jnp.concatenate(
        [tall[pl.ds(j, n * parts, stride=per), :][:, :own] for j in range(per)], axis=1
    )
    for d in range(n):
        fbuf[d] = packed[d * parts : (d + 1) * parts]

    def f_copy(sender, pr, pc, dest):
        return pltpu.make_async_remote_copy(
            src_ref=fbuf.at[dest],
            dst_ref=fr.at[sender],
            send_sem=f_send.at[dest],
            recv_sem=f_recv.at[sender],
            device_id=(pr, pc),
            device_id_type=MESH,
        )

    @pl.loop(1, n)
    def _(step):
        pr, pc, dest = partner(step)
        f_copy(me, pr, pc, dest).start()

    fr[me] = fbuf[me]

    @pl.loop(left, n)
    def _(step):
        pr, pc, dest = partner(step)
        t_copy(me, pr, pc, dest).wait_send()

    @pl.loop(1, cols)
    def _(step):
        _, pc, _ = partner(step)
        w_copy(c, pc).wait_send()

    for mask in order:
        if mask:
            c_copy(c, flip(c, mask, cols)).wait_send()

    @pl.loop(0, cols)
    def _(pc):
        for i in range(1, rows):
            r_copy(pc, r, core, (r + i) % rows).wait_send()

        @pl.when(pc % 2 != core)
        def _():
            r_copy(pc, r, core, r).wait_send()

    @pl.loop(1, n)
    def _(step):
        pr, pc, source = partner(step)
        f_copy(source, pr, pc, me).wait_recv()

    for d in range(n):
        flat[d * parts : (d + 1) * parts, :] = fr[d]
    got = flat[...]
    for j in range(per):
        tall[pl.ds(j, n * parts, stride=per), :] = jnp.pad(
            got[:, j * own : (j + 1) * own], ((0, 0), (0, 128 - own))
        )
    across = jnp.concatenate([tall[d * own : (d + 1) * own, :own] for d in range(n)], axis=1)
    out_ref[...] = full + across

    @pl.loop(1, n)
    def _(step):
        pr, pc, dest = partner(step)
        f_copy(me, pr, pc, dest).wait_send()


def in_one_kernel(multiplier, cycle_tiles):
    own, width = multiplier.shape
    rows, cols = lax.axis_size("row"), lax.axis_size("col")
    n = rows * cols
    block, chunk, count = width // n, cycle_tiles.shape[1], own * n
    parts = own * own // 128
    f32, bf16 = jnp.float32, jnp.bfloat16
    dma = pltpu.SemaphoreType.DMA
    return pl.pallas_call(
        functools.partial(cycle_kernel, rows, cols),
        out_shape=jax.ShapeDtypeStruct((own, count), f32),
        in_specs=[pl.BlockSpec(memory_space=pltpu.HBM)] * 2,
        out_specs=pl.BlockSpec(memory_space=pltpu.VMEM),
        scratch_shapes=[
            pltpu.VMEM((own, width), f32),
            pltpu.VMEM((count, block), f32),
            pltpu.VMEM((own * count, 128), f32),
            pltpu.VMEM((count, block), f32),
            pltpu.VMEM((count, block), bf16),
            pltpu.VMEM((count, block), bf16),
            pltpu.VMEM((cols, chunk, block), f32),
            pltpu.VMEM((cols, chunk, count), f32),
            pltpu.VMEM((cols // 2, rows, 2, own, count), f32),
            pltpu.VMEM((cols // 2, own, count), f32),
            pltpu.VMEM((cols // 2, own, count), f32),
            pltpu.VMEM((count, 128), f32),
            pltpu.VMEM((n, parts, 128), f32),
            pltpu.VMEM((n, parts, 128), f32),
            pltpu.VMEM((n * parts, 128), f32),
            dma((2,)), dma((n,)), dma((n,)), dma((cols,)), dma((cols,)),
            dma((cols, rows)), dma((cols // 2, rows, 2)),
            dma((cols // 2,)), dma((cols // 2,)), dma((n,)), dma((n,)),
        ],
        compiler_params=pltpu.CompilerParams(
            collective_id=0, has_side_effects=True, vmem_limit_bytes=62 * 1024 * 1024
        ),
        cost_estimate=pl.CostEstimate(
            flops=6 * count * block * count, bytes_accessed=4 * own * width, transcendentals=0
        ),
    )(multiplier, cycle_tiles.T)


def in_collectives(multiplier, cycle_tiles):
    rows_loc, full_width = multiplier.shape
    row_count = lax.axis_size("row")
    col_count = lax.axis_size("col")
    devices = row_count * col_count
    block_width = full_width // devices
    out_block = cycle_tiles.shape[1] // row_count
    virt_dev = rows_loc // OW
    all_rows = rows_loc * devices
    pieces = multiplier.reshape(1, rows_loc, devices, block_width)
    moved = lax.all_to_all(pieces, ("row", "col"), split_axis=2, concat_axis=0, tiled=True)
    direct = moved.reshape(all_rows, block_width)
    cycle_rows = lax.all_to_all(cycle_tiles.T, "col", split_axis=1, concat_axis=0, tiled=True)
    swapped = jnp.transpose(multiplier.reshape(virt_dev, OW, V, O), (2, 1, 0, 3)).reshape(
        all_rows, block_width
    )
    combined = 2.0 * direct - swapped
    partial_value = lax.dot_general(
        cycle_rows,
        combined,
        (((1,), (1,)), ((), ())),
        precision=lax.Precision.HIGHEST,
        preferred_element_type=jnp.float32,
    )
    partial_value = partial_value.reshape(col_count, row_count, out_block, all_rows)
    over_row = lax.psum_scatter(partial_value, "row", scatter_dimension=1, tiled=True)
    own_cols = lax.psum_scatter(over_row, "col", scatter_dimension=0, tiled=True)
    own_cols = own_cols.reshape(out_block, all_rows)
    outgoing = own_cols.reshape(1, out_block, devices, rows_loc)
    arrived = lax.all_to_all(outgoing, ("row", "col"), split_axis=2, concat_axis=0, tiled=True)
    own_rows = arrived.reshape(devices * out_block, rows_loc).T
    return own_rows + own_cols


def on_device(multiplier, cycle_tiles):
    own, width = multiplier.shape
    rows, cols = lax.axis_size("row"), lax.axis_size("col")
    block = width // (rows * cols)
    powers = rows & (rows - 1) == 0 and cols & (cols - 1) == 0
    whole_tiles = own % 16 == 0 and 128 % own == 0 and block % 128 == 0 and cols > 1
    if OW == 1 and O <= 128 and powers and whole_tiles and block == own * O:
        return in_one_kernel(multiplier, cycle_tiles)
    return in_collectives(multiplier, cycle_tiles)


def solution(mesh):
    placed = (P(("row", "col"), None), P("row", "col"))
    return jax.shard_map(
        on_device, mesh=mesh, in_specs=placed, out_specs=P(("row", "col"), None), check_vma=False
    )
```

```python
import functools

import jax
import jax.numpy as jnp
from jax import lax
from jax.experimental import pallas as pl
from jax.experimental.pallas import tpu as pltpu
from jax.sharding import PartitionSpec as P

O = 40
V = 512
OW = 1
MESH = pl.DeviceIdType.MESH


def flip(x, y, size):
    total, bit = 0, 1
    while bit < size:
        total = total + bit * ((x // bit + y // bit) % 2)
        bit *= 2
    return total


def halves(x):
    high = x.astype(jnp.bfloat16)
    return high, (x - high.astype(jnp.float32)).astype(jnp.bfloat16)


def dot_nt(x, y):
    return lax.dot_general(
        x, y, (((1,), (1,)), ((), ())), preferred_element_type=jnp.float32
    )


def cycle_kernel(
    rows, cols, t_hbm, w_hbm, out_ref,
    t_ref, tdir, u, sw, dh, dl, wr, pbuf, rbuf, qbuf, cbuf, tall, fbuf, fr, flat,
    here, t_send, t_recv, w_send, w_recv, r_send, r_recv, c_send, c_recv, f_send, f_recv,
):
    n = rows * cols
    own, width = t_ref.shape
    block = width // n
    chunk = w_hbm.shape[0]
    count = own * n
    r = lax.axis_index("row")
    c = lax.axis_index("col")
    me = r * cols + c

    core = c % 2
    t_here = pltpu.make_async_copy(t_hbm, t_ref, here.at[0])
    t_here.start()
    w_here = pltpu.make_async_copy(
        w_hbm.at[:, pl.ds(pl.multiple_of(c * block, 128), block)], wr.at[c], here.at[1]
    )
    w_here.start()

    def mask_of(step):
        s = step % cols
        return (s % 2) * (cols // 2) + s // 2

    def partner(step):
        s, q = step % cols, step // cols
        pr = flip(r, (q + s) % rows, rows)
        pc = flip(c, mask_of(step), cols)
        return pr, pc, pr * cols + pc

    barrier = pltpu.get_barrier_semaphore()

    @pl.loop(1, n)
    def _(step):
        pr, pc, _ = partner(step)
        pl.semaphore_signal(barrier, inc=1, device_id=(pr, pc), device_id_type=MESH)

    pl.semaphore_wait(barrier, n - 1)

    def t_copy(sender, pr, pc, dest):
        return pltpu.make_async_remote_copy(
            src_ref=t_hbm.at[:, pl.ds(pl.multiple_of(dest * block, 128), block)],
            dst_ref=tdir.at[pl.ds(pl.multiple_of(sender * own, own), own), :],
            send_sem=t_send.at[dest],
            recv_sem=t_recv.at[sender],
            device_id=(pr, pc),
            device_id_type=MESH,
        )

    def t_start(step):
        pr, pc, dest = partner(step)
        t_copy(me, pr, pc, dest).start()

    def t_far():
        pl.loop(0, n // 2)(lambda i: t_start(2 * i + 1))

    pl.when(core == 0)(t_far)
    pl.loop(1, n // 2)(lambda i: t_start(2 * i))
    pl.when(core == 1)(t_far)

    def w_copy(sender, dest):
        return pltpu.make_async_remote_copy(
            src_ref=w_hbm.at[:, pl.ds(pl.multiple_of(dest * block, 128), block)],
            dst_ref=wr.at[sender],
            send_sem=w_send.at[dest],
            recv_sem=w_recv.at[sender],
            device_id=(r, dest),
            device_id_type=MESH,
        )

    half = cols // 2

    def w_start(i):
        far_first = i - 1 + half
        far_first = far_first - far_first // cols * (cols - 1)
        w_copy(c, flip(c, far_first + core * (i - far_first), cols)).start()

    w_start(1)
    w_start(2)
    t_here.wait()
    tdir[pl.ds(pl.multiple_of(me * own, own), own), :] = t_ref[
        :, pl.ds(pl.multiple_of(me * block, 128), block)
    ]

    @pl.loop(0, n)
    def _(part):
        x = t_ref[:, pl.ds(pl.multiple_of(part * block, 128), block)]
        for j in range(own):
            piece = jnp.pad(x[:, j * O : (j + 1) * O], ((0, 0), (0, 128 - O)))
            for half in range(0, own, 8):
                u[pl.ds(half * count + part * own + j, 8, stride=count), :] = piece[
                    half : half + 8
                ]

    for j in range(own):
        sw[:, j * O : (j + 1) * O] = u[j * count : (j + 1) * count, 0:O]

    def combine(source):
        at = pl.ds(pl.multiple_of(source * own, own), own)
        high, low = halves(2.0 * tdir[at, :] - sw[at, :])
        dh[at, :] = high
        dl[at, :] = low

    combine(me)

    @pl.loop(1, n)
    def _(step):
        pr, pc, source = partner(step)
        t_copy(source, pr, pc, me).wait_recv()
        combine(source)

    def r_copy(pc, sender_row, sender_core, dest):
        return pltpu.make_async_remote_copy(
            src_ref=pbuf.at[pc, pl.ds(pl.multiple_of(dest * own, own), own), :],
            dst_ref=rbuf.at[pc // 2, sender_row, sender_core],
            send_sem=r_send.at[pc, dest],
            recv_sem=r_recv.at[pc // 2, sender_row, sender_core],
            device_id=(dest, c - core + pc % 2),
            device_id_type=MESH,
        )

    def c_copy(sender, dest):
        return pltpu.make_async_remote_copy(
            src_ref=qbuf.at[dest // 2],
            dst_ref=cbuf.at[sender // 2],
            send_sem=c_send.at[dest // 2],
            recv_sem=c_recv.at[sender // 2],
            device_id=(r, dest),
            device_id_type=MESH,
        )

    def multiply(pc):
        high, low = halves(wr[pc])
        both = dot_nt(jnp.concatenate([high, low], axis=0), dh[...])
        pbuf[pc] = both[:chunk] + both[chunk:] + dot_nt(high, dl[...])
        for i in range(1, rows):
            r_copy(pc, r, core, (r + i) % rows).start()

        @pl.when(pc % 2 != core)
        def _():
            r_copy(pc, r, core, r).start()

    def collect(pc):
        total = pbuf[pc, pl.ds(pl.multiple_of(r * own, own), own), :]
        for i in range(rows):
            for k in range(2):
                if i or k:
                    sender, side = (r + i) % rows, (core + k) % 2
                    r_copy(pc, sender, side, r).wait_recv()
                    total = total + rbuf[pc // 2, sender, side]
        qbuf[pc // 2] = total

    near = [[m for m in range(1, half) if m % 2 == k] for k in range(2)]
    far = [[m for m in range(half, cols) if m % 2 == k] for k in range(2)]
    orders = [
        [0] + early + first + second[:-1] + late + second[-1:]
        for early, first, second, late in (
            (near[1], far[0], far[1], near[0]),
            (near[0], far[1], far[0], near[1]),
        )
    ]
    codes = [sum(m * cols**i for i, m in enumerate(o)) for o in orders]
    ready = {
        m: [max(orders[k].index(m), orders[1 - k].index(m + 1)) + 1 for k in range(2)]
        for m in range(0, cols, 2)
    }
    order = sorted(ready, key=lambda m: max(ready[m]))

    def collect_mask(mask):
        pc = flip(c, mask, cols)
        collect(pc)
        if mask:
            c_copy(c, pc).start()

    w_here.wait()
    multiply(c)

    def chunk_step(step, code):
        pc = flip(c, code % cols, cols)
        w_copy(pc, c).wait_recv()
        pl.when(step + 2 < cols)(lambda: w_start(step + 2))
        multiply(pc)
        for mask in order:
            first, second = ready[mask]
            pl.when(step == first + core * (second - first))(
                functools.partial(collect_mask, mask)
            )
        return code // cols

    code = codes[0] + core * (codes[1] - codes[0])
    lax.fori_loop(1, cols, chunk_step, code // cols)

    for mask in order:
        for k in range(2):
            if ready[mask][k] >= cols:
                pl.when(core == k)(functools.partial(collect_mask, mask))

    full = qbuf[c // 2]
    for mask in order:
        if mask:
            pc = flip(c, mask, cols)
            c_copy(pc, c).wait_recv()
            full = full + cbuf[pc // 2]

    per = 128 // own
    parts = own // per
    tall[...] = jnp.pad(full.T, ((0, 0), (0, 128 - own)))
    packed = jnp.concatenate(
        [tall[pl.ds(j, n * parts, stride=per), :][:, :own] for j in range(per)], axis=1
    )
    for d in range(n):
        fbuf[d] = packed[d * parts : (d + 1) * parts]

    def f_copy(sender, pr, pc, dest):
        return pltpu.make_async_remote_copy(
            src_ref=fbuf.at[dest],
            dst_ref=fr.at[sender],
            send_sem=f_send.at[dest],
            recv_sem=f_recv.at[sender],
            device_id=(pr, pc),
            device_id_type=MESH,
        )

    @pl.loop(1, n)
    def _(step):
        pr, pc, dest = partner(step)
        f_copy(me, pr, pc, dest).start()

    fr[me] = fbuf[me]

    @pl.loop(1, n)
    def _(step):
        pr, pc, dest = partner(step)
        t_copy(me, pr, pc, dest).wait_send()

    @pl.loop(1, cols)
    def _(step):
        _, pc, _ = partner(step)
        w_copy(c, pc).wait_send()

    for mask in order:
        if mask:
            c_copy(c, flip(c, mask, cols)).wait_send()

    @pl.loop(0, cols)
    def _(pc):
        for i in range(1, rows):
            r_copy(pc, r, core, (r + i) % rows).wait_send()

        @pl.when(pc % 2 != core)
        def _():
            r_copy(pc, r, core, r).wait_send()

    @pl.loop(1, n)
    def _(step):
        pr, pc, source = partner(step)
        f_copy(source, pr, pc, me).wait_recv()

    for d in range(n):
        flat[d * parts : (d + 1) * parts, :] = fr[d]
    got = flat[...]
    for j in range(per):
        tall[pl.ds(j, n * parts, stride=per), :] = jnp.pad(
            got[:, j * own : (j + 1) * own], ((0, 0), (0, 128 - own))
        )
    across = jnp.concatenate([tall[d * own : (d + 1) * own, :own] for d in range(n)], axis=1)
    out_ref[...] = full + across

    @pl.loop(1, n)
    def _(step):
        pr, pc, dest = partner(step)
        f_copy(me, pr, pc, dest).wait_send()


def in_one_kernel(multiplier, cycle_tiles):
    own, width = multiplier.shape
    rows, cols = lax.axis_size("row"), lax.axis_size("col")
    n = rows * cols
    block, chunk, count = width // n, cycle_tiles.shape[1], own * n
    parts = own * own // 128
    f32, bf16 = jnp.float32, jnp.bfloat16
    dma = pltpu.SemaphoreType.DMA
    return pl.pallas_call(
        functools.partial(cycle_kernel, rows, cols),
        out_shape=jax.ShapeDtypeStruct((own, count), f32),
        in_specs=[pl.BlockSpec(memory_space=pltpu.HBM)] * 2,
        out_specs=pl.BlockSpec(memory_space=pltpu.VMEM),
        scratch_shapes=[
            pltpu.VMEM((own, width), f32),
            pltpu.VMEM((count, block), f32),
            pltpu.VMEM((own * count, 128), f32),
            pltpu.VMEM((count, block), f32),
            pltpu.VMEM((count, block), bf16),
            pltpu.VMEM((count, block), bf16),
            pltpu.VMEM((cols, chunk, block), f32),
            pltpu.VMEM((cols, chunk, count), f32),
            pltpu.VMEM((cols // 2, rows, 2, own, count), f32),
            pltpu.VMEM((cols // 2, own, count), f32),
            pltpu.VMEM((cols // 2, own, count), f32),
            pltpu.VMEM((count, 128), f32),
            pltpu.VMEM((n, parts, 128), f32),
            pltpu.VMEM((n, parts, 128), f32),
            pltpu.VMEM((n * parts, 128), f32),
            dma((2,)), dma((n,)), dma((n,)), dma((cols,)), dma((cols,)),
            dma((cols, rows)), dma((cols // 2, rows, 2)),
            dma((cols // 2,)), dma((cols // 2,)), dma((n,)), dma((n,)),
        ],
        compiler_params=pltpu.CompilerParams(
            collective_id=0, has_side_effects=True, vmem_limit_bytes=62 * 1024 * 1024
        ),
        cost_estimate=pl.CostEstimate(
            flops=6 * count * block * count, bytes_accessed=4 * own * width, transcendentals=0
        ),
    )(multiplier, cycle_tiles.T)


def in_collectives(multiplier, cycle_tiles):
    rows_loc, full_width = multiplier.shape
    row_count = lax.axis_size("row")
    col_count = lax.axis_size("col")
    devices = row_count * col_count
    block_width = full_width // devices
    out_block = cycle_tiles.shape[1] // row_count
    virt_dev = rows_loc // OW
    all_rows = rows_loc * devices
    pieces = multiplier.reshape(1, rows_loc, devices, block_width)
    moved = lax.all_to_all(pieces, ("row", "col"), split_axis=2, concat_axis=0, tiled=True)
    direct = moved.reshape(all_rows, block_width)
    cycle_rows = lax.all_to_all(cycle_tiles.T, "col", split_axis=1, concat_axis=0, tiled=True)
    swapped = jnp.transpose(multiplier.reshape(virt_dev, OW, V, O), (2, 1, 0, 3)).reshape(
        all_rows, block_width
    )
    combined = 2.0 * direct - swapped
    partial_value = lax.dot_general(
        cycle_rows,
        combined,
        (((1,), (1,)), ((), ())),
        precision=lax.Precision.HIGHEST,
        preferred_element_type=jnp.float32,
    )
    partial_value = partial_value.reshape(col_count, row_count, out_block, all_rows)
    over_row = lax.psum_scatter(partial_value, "row", scatter_dimension=1, tiled=True)
    own_cols = lax.psum_scatter(over_row, "col", scatter_dimension=0, tiled=True)
    own_cols = own_cols.reshape(out_block, all_rows)
    outgoing = own_cols.reshape(1, out_block, devices, rows_loc)
    arrived = lax.all_to_all(outgoing, ("row", "col"), split_axis=2, concat_axis=0, tiled=True)
    own_rows = arrived.reshape(devices * out_block, rows_loc).T
    return own_rows + own_cols


def on_device(multiplier, cycle_tiles):
    own, width = multiplier.shape
    rows, cols = lax.axis_size("row"), lax.axis_size("col")
    block = width // (rows * cols)
    powers = rows & (rows - 1) == 0 and cols & (cols - 1) == 0
    whole_tiles = own % 16 == 0 and 128 % own == 0 and block % 128 == 0 and 4 <= cols <= 8
    if OW == 1 and O <= 128 and powers and whole_tiles and block == own * O:
        return in_one_kernel(multiplier, cycle_tiles)
    return in_collectives(multiplier, cycle_tiles)


def solution(mesh):
    placed = (P(("row", "col"), None), P("row", "col"))
    return jax.shard_map(
        on_device, mesh=mesh, in_specs=placed, out_specs=P(("row", "col"), None), check_vma=False
    )
```

```python
import functools

import jax
import jax.numpy as jnp
from jax import lax
from jax.experimental import pallas as pl
from jax.experimental.pallas import tpu as pltpu
from jax.sharding import PartitionSpec as P

O = 40
V = 512
OW = 1
MESH = pl.DeviceIdType.MESH


def flip(x, y, size):
    total, bit = 0, 1
    while bit < size:
        total = total + bit * ((x // bit + y // bit) % 2)
        bit *= 2
    return total


def halves(x):
    high = x.astype(jnp.bfloat16)
    return high, (x - high.astype(jnp.float32)).astype(jnp.bfloat16)


def dot_nt(x, y):
    return lax.dot_general(
        x, y, (((1,), (1,)), ((), ())), preferred_element_type=jnp.float32
    )


def cycle_kernel(
    rows, cols, t_hbm, w_hbm, out_ref,
    t_ref, tdir, u, sw, dh, dl, wr, pbuf, rbuf, qbuf, cbuf, tall, fbuf, fr, flat,
    here, t_send, t_recv, w_send, w_recv, r_send, r_recv, c_send, c_recv, f_send, f_recv,
):
    n = rows * cols
    own, width = t_ref.shape
    block = width // n
    chunk = w_hbm.shape[0]
    count = own * n
    r = lax.axis_index("row")
    c = lax.axis_index("col")
    me = r * cols + c

    core = c % 2
    t_here = pltpu.make_async_copy(t_hbm, t_ref, here.at[0])
    t_here.start()
    w_here = pltpu.make_async_copy(
        w_hbm.at[:, pl.ds(pl.multiple_of(c * block, 128), block)], wr.at[c], here.at[1]
    )
    w_here.start()

    def mask_of(step):
        s = step % cols
        return (s % 2) * (cols // 2) + s // 2

    def partner(step):
        s, q = step % cols, step // cols
        pr = flip(r, (q + s) % rows, rows)
        pc = flip(c, mask_of(step), cols)
        return pr, pc, pr * cols + pc

    barrier = pltpu.get_barrier_semaphore()

    @pl.loop(1, n)
    def _(step):
        pr, pc, _ = partner(step)
        pl.semaphore_signal(barrier, inc=1, device_id=(pr, pc), device_id_type=MESH)

    pl.semaphore_wait(barrier, n - 1)

    def t_copy(sender, pr, pc, dest):
        return pltpu.make_async_remote_copy(
            src_ref=t_hbm.at[:, pl.ds(pl.multiple_of(dest * block, 128), block)],
            dst_ref=tdir.at[pl.ds(pl.multiple_of(sender * own, own), own), :],
            send_sem=t_send.at[dest],
            recv_sem=t_recv.at[sender],
            device_id=(pr, pc),
            device_id_type=MESH,
        )

    @pl.loop(1, n)
    def _(step):
        pr, pc, dest = partner(step)
        t_copy(me, pr, pc, dest).start()

    def w_copy(sender, dest):
        return pltpu.make_async_remote_copy(
            src_ref=w_hbm.at[:, pl.ds(pl.multiple_of(dest * block, 128), block)],
            dst_ref=wr.at[sender],
            send_sem=w_send.at[dest],
            recv_sem=w_recv.at[sender],
            device_id=(r, dest),
            device_id_type=MESH,
        )

    t_here.wait()
    tdir[pl.ds(pl.multiple_of(me * own, own), own), :] = t_ref[
        :, pl.ds(pl.multiple_of(me * block, 128), block)
    ]

    @pl.loop(0, n)
    def _(part):
        x = t_ref[:, pl.ds(pl.multiple_of(part * block, 128), block)]
        for j in range(own):
            piece = jnp.pad(x[:, j * O : (j + 1) * O], ((0, 0), (0, 128 - O)))
            for half in range(0, own, 8):
                u[pl.ds(half * count + part * own + j, 8, stride=count), :] = piece[
                    half : half + 8
                ]

    for j in range(own):
        sw[:, j * O : (j + 1) * O] = u[j * count : (j + 1) * count, 0:O]

    def combine(source):
        at = pl.ds(pl.multiple_of(source * own, own), own)
        high, low = halves(2.0 * tdir[at, :] - sw[at, :])
        dh[at, :] = high
        dl[at, :] = low

    left = n - n // 8

    @pl.loop(1, left)
    def _(step):
        pr, pc, dest = partner(step)
        t_copy(me, pr, pc, dest).wait_send()

    @pl.loop(1, cols)
    def _(step):
        _, pc, _ = partner(step)
        w_copy(c, pc).start()

    combine(me)

    @pl.loop(1, n)
    def _(step):
        pr, pc, source = partner(step)
        t_copy(source, pr, pc, me).wait_recv()
        combine(source)

    def r_copy(pc, sender_row, sender_core, dest):
        return pltpu.make_async_remote_copy(
            src_ref=pbuf.at[pc, pl.ds(pl.multiple_of(dest * own, own), own), :],
            dst_ref=rbuf.at[pc // 2, sender_row, sender_core],
            send_sem=r_send.at[pc, dest],
            recv_sem=r_recv.at[pc // 2, sender_row, sender_core],
            device_id=(dest, c - core + pc % 2),
            device_id_type=MESH,
        )

    def c_copy(sender, dest):
        return pltpu.make_async_remote_copy(
            src_ref=qbuf.at[dest // 2],
            dst_ref=cbuf.at[sender // 2],
            send_sem=c_send.at[dest // 2],
            recv_sem=c_recv.at[sender // 2],
            device_id=(r, dest),
            device_id_type=MESH,
        )

    def multiply(pc):
        high, low = halves(wr[pc])
        both = dot_nt(jnp.concatenate([high, low], axis=0), dh[...])
        pbuf[pc] = both[:chunk] + both[chunk:] + dot_nt(high, dl[...])
        for i in range(1, rows):
            r_copy(pc, r, core, (r + i) % rows).start()

        @pl.when(pc % 2 != core)
        def _():
            r_copy(pc, r, core, r).start()

    def collect(pc):
        total = pbuf[pc, pl.ds(pl.multiple_of(r * own, own), own), :]
        for i in range(rows):
            for k in range(2):
                if i or k:
                    sender, side = (r + i) % rows, (core + k) % 2
                    r_copy(pc, sender, side, r).wait_recv()
                    total = total + rbuf[pc // 2, sender, side]
        qbuf[pc // 2] = total

    steps = [mask_of(step) for step in range(cols)]
    ready = {m: max(steps.index(m), steps.index(m + 1)) + 1 for m in range(0, cols, 2)}
    order = sorted(ready, key=lambda m: ready[m])

    def collect_mask(mask):
        pc = flip(c, mask, cols)
        collect(pc)
        if mask:
            c_copy(c, pc).start()

    w_here.wait()
    multiply(c)

    @pl.loop(1, cols)
    def _(step):
        _, pc, _ = partner(step)
        for mask in order:
            if ready[mask] < cols:
                pl.when(step == ready[mask])(functools.partial(collect_mask, mask))
        w_copy(pc, c).wait_recv()
        multiply(pc)

    for mask in order:
        if ready[mask] >= cols:
            collect_mask(mask)

    full = qbuf[c // 2]
    for mask in order:
        if mask:
            pc = flip(c, mask, cols)
            c_copy(pc, c).wait_recv()
            full = full + cbuf[pc // 2]

    per = 128 // own
    parts = own // per
    tall[...] = jnp.pad(full.T, ((0, 0), (0, 128 - own)))
    packed = jnp.concatenate(
        [tall[pl.ds(j, n * parts, stride=per), :][:, :own] for j in range(per)], axis=1
    )
    for d in range(n):
        fbuf[d] = packed[d * parts : (d + 1) * parts]

    def f_copy(sender, pr, pc, dest):
        return pltpu.make_async_remote_copy(
            src_ref=fbuf.at[dest],
            dst_ref=fr.at[sender],
            send_sem=f_send.at[dest],
            recv_sem=f_recv.at[sender],
            device_id=(pr, pc),
            device_id_type=MESH,
        )

    @pl.loop(1, n)
    def _(step):
        pr, pc, dest = partner(step)
        f_copy(me, pr, pc, dest).start()

    fr[me] = fbuf[me]

    @pl.loop(left, n)
    def _(step):
        pr, pc, dest = partner(step)
        t_copy(me, pr, pc, dest).wait_send()

    @pl.loop(1, cols)
    def _(step):
        _, pc, _ = partner(step)
        w_copy(c, pc).wait_send()

    for mask in order:
        if mask:
            c_copy(c, flip(c, mask, cols)).wait_send()

    @pl.loop(0, cols)
    def _(pc):
        for i in range(1, rows):
            r_copy(pc, r, core, (r + i) % rows).wait_send()

        @pl.when(pc % 2 != core)
        def _():
            r_copy(pc, r, core, r).wait_send()

    @pl.loop(1, n)
    def _(step):
        pr, pc, source = partner(step)
        f_copy(source, pr, pc, me).wait_recv()

    for d in range(n):
        flat[d * parts : (d + 1) * parts, :] = fr[d]
    got = flat[...]
    for j in range(per):
        tall[pl.ds(j, n * parts, stride=per), :] = jnp.pad(
            got[:, j * own : (j + 1) * own], ((0, 0), (0, 128 - own))
        )
    across = jnp.concatenate([tall[d * own : (d + 1) * own, :own] for d in range(n)], axis=1)
    out_ref[...] = full + across

    @pl.loop(1, n)
    def _(step):
        pr, pc, dest = partner(step)
        f_copy(me, pr, pc, dest).wait_send()


def in_one_kernel(multiplier, cycle_tiles):
    own, width = multiplier.shape
    rows, cols = lax.axis_size("row"), lax.axis_size("col")
    n = rows * cols
    block, chunk, count = width // n, cycle_tiles.shape[1], own * n
    parts = own * own // 128
    f32, bf16 = jnp.float32, jnp.bfloat16
    dma = pltpu.SemaphoreType.DMA
    return pl.pallas_call(
        functools.partial(cycle_kernel, rows, cols),
        out_shape=jax.ShapeDtypeStruct((own, count), f32),
        in_specs=[pl.BlockSpec(memory_space=pltpu.HBM)] * 2,
        out_specs=pl.BlockSpec(memory_space=pltpu.VMEM),
        scratch_shapes=[
            pltpu.VMEM((own, width), f32),
            pltpu.VMEM((count, block), f32),
            pltpu.VMEM((own * count, 128), f32),
            pltpu.VMEM((count, block), f32),
            pltpu.VMEM((count, block), bf16),
            pltpu.VMEM((count, block), bf16),
            pltpu.VMEM((cols, chunk, block), f32),
            pltpu.VMEM((cols, chunk, count), f32),
            pltpu.VMEM((cols // 2, rows, 2, own, count), f32),
            pltpu.VMEM((cols // 2, own, count), f32),
            pltpu.VMEM((cols // 2, own, count), f32),
            pltpu.VMEM((count, 128), f32),
            pltpu.VMEM((n, parts, 128), f32),
            pltpu.VMEM((n, parts, 128), f32),
            pltpu.VMEM((n * parts, 128), f32),
            dma((2,)), dma((n,)), dma((n,)), dma((cols,)), dma((cols,)),
            dma((cols, rows)), dma((cols // 2, rows, 2)),
            dma((cols // 2,)), dma((cols // 2,)), dma((n,)), dma((n,)),
        ],
        compiler_params=pltpu.CompilerParams(
            collective_id=0, has_side_effects=True, vmem_limit_bytes=62 * 1024 * 1024
        ),
        cost_estimate=pl.CostEstimate(
            flops=6 * count * block * count, bytes_accessed=4 * own * width, transcendentals=0
        ),
    )(multiplier, cycle_tiles.T)


def in_collectives(multiplier, cycle_tiles):
    rows_loc, full_width = multiplier.shape
    row_count = lax.axis_size("row")
    col_count = lax.axis_size("col")
    devices = row_count * col_count
    block_width = full_width // devices
    out_block = cycle_tiles.shape[1] // row_count
    virt_dev = rows_loc // OW
    all_rows = rows_loc * devices
    pieces = multiplier.reshape(1, rows_loc, devices, block_width)
    moved = lax.all_to_all(pieces, ("row", "col"), split_axis=2, concat_axis=0, tiled=True)
    direct = moved.reshape(all_rows, block_width)
    cycle_rows = lax.all_to_all(cycle_tiles.T, "col", split_axis=1, concat_axis=0, tiled=True)
    swapped = jnp.transpose(multiplier.reshape(virt_dev, OW, V, O), (2, 1, 0, 3)).reshape(
        all_rows, block_width
    )
    combined = 2.0 * direct - swapped
    partial_value = lax.dot_general(
        cycle_rows,
        combined,
        (((1,), (1,)), ((), ())),
        precision=lax.Precision.HIGHEST,
        preferred_element_type=jnp.float32,
    )
    partial_value = partial_value.reshape(col_count, row_count, out_block, all_rows)
    over_row = lax.psum_scatter(partial_value, "row", scatter_dimension=1, tiled=True)
    own_cols = lax.psum_scatter(over_row, "col", scatter_dimension=0, tiled=True)
    own_cols = own_cols.reshape(out_block, all_rows)
    outgoing = own_cols.reshape(1, out_block, devices, rows_loc)
    arrived = lax.all_to_all(outgoing, ("row", "col"), split_axis=2, concat_axis=0, tiled=True)
    own_rows = arrived.reshape(devices * out_block, rows_loc).T
    return own_rows + own_cols


def on_device(multiplier, cycle_tiles):
    own, width = multiplier.shape
    rows, cols = lax.axis_size("row"), lax.axis_size("col")
    block = width // (rows * cols)
    powers = rows & (rows - 1) == 0 and cols & (cols - 1) == 0
    whole_tiles = own % 16 == 0 and 128 % own == 0 and block % 128 == 0 and cols > 1
    if OW == 1 and O <= 128 and powers and whole_tiles and block == own * O:
        return in_one_kernel(multiplier, cycle_tiles)
    return in_collectives(multiplier, cycle_tiles)


def solution(mesh):
    placed = (P(("row", "col"), None), P("row", "col"))
    return jax.shard_map(
        on_device, mesh=mesh, in_specs=placed, out_specs=P(("row", "col"), None), check_vma=False
    )
```
